256 devices in a mesh: ctx: 16 (over x, z_lo), tp: 16 (over z_hi, y, core).
Axes of the slice: x: 4, y: 4, z: 8 (z_hi: 2, z_lo: 4; z = z_hi * 4 + z_lo), core: 2. Of those that a mesh axis runs over, the one named last changes fastest.
Arguments:
- tokens: bfloat16 [16384, 2048], P('ctx', 'tp'), may hold values from -600 to 600
- gain: bfloat16 [2048], P('tp'), may hold values from 0.25 to 1.75
- w_inputs: bfloat16 [2048, 2048], P(None, 'tp'), may hold values from -0.125 to 0.125
- filters: float32 [24, 16384], P(None, 'ctx'), may hold values from -0.078125 to 0.078125
- w_plus: bfloat16 [24, 2048], P(None, 'tp'), may hold values from -1.25 to 1.25
- w_minus: bfloat16 [24, 2048], P(None, 'tp'), may hold values from -1.25 to 1.25
Outputs:
- mixed: bfloat16 [16384, 2048], P('ctx', 'tp')
The draws below stay inside these ranges and needn't reach their ends.
All inputs are finite; a program needn't handle non-finite values.
Results may differ from the reference program's by a relative error of at most 0.0049.
Values may be sent and summed in bfloat16 or wider, within the bound.
No kernel may reach another device: no remote copies, remote signals or barrier semaphores. Data moves between devices by JAX's collectives and lax.ppermute only.
A program may use at most 64 MiB of HBM per device.

```python
import math
import jax
import jax.numpy as jnp
from jax import lax

D = 2048
K = 24
SEQ = 16384


def draw_tokens(key, part):
    key = jax.random.fold_in(key, 11)
    key_base, key_rows, key_cols = jax.random.split(key, 3)
    feature = jnp.arange(D, dtype=jnp.float32) / D
    jitter = jnp.exp(jax.random.uniform(key_cols, (D,), jnp.float32, -0.35, 0.35))
    base = jnp.clip(jax.random.normal(key_base, (SEQ, D), jnp.float32), -6.0, 6.0)
    row_scale = jnp.exp(jax.random.uniform(key_rows, (SEQ, 1), jnp.float32, 0.0, math.log(10.0)))
    col_scale = 0.3 * jnp.exp(feature * math.log(10.0)) * jitter
    return (row_scale * base * col_scale[None, :]).astype(jnp.bfloat16)


def shard_levels(stream_key, dims, shards, smallest, largest):
    level, own = 1.0, jax.random.fold_in(stream_key, 6)
    for axis_at, parts in shards:
        heights = jnp.exp(jax.random.uniform(jax.random.fold_in(own, axis_at), (parts,), jnp.float32, smallest / len(shards), largest / len(shards)))
        level = level * jnp.repeat(heights, dims[axis_at] // parts).reshape([-1 if axis == axis_at else 1 for axis in range(len(dims))])
    return level


def normal_values(key, shape, scale, limit, pieces=(), kind=jnp.bfloat16):
    drawn = jax.random.normal(key, shape, jnp.float32) * scale
    if len(pieces) > 0:
        drawn = shard_levels(key, shape, pieces, -0.22, 0.18) * drawn
    return jnp.clip(drawn, min=-limit, max=limit).astype(kind)


def setup_inputs(seed: int = 0) -> dict:
    streams_of = jax.random.split(jax.random.key(seed), 7)
    tokens = draw_tokens(jax.random.fold_in(streams_of[6], 71), 0)
    gain = jnp.clip(1.0 + 0.15 * jax.random.normal(streams_of[1], (D,), jnp.float32), 0.25, 1.75).astype(jnp.bfloat16)
    w_inputs = normal_values(streams_of[2], (D, D), D ** -0.5, 0.125, ((1, 16),))
    filters = normal_values(streams_of[3], (K, SEQ), ((2 * SEQ) ** -0.5), 0.078125, ((1, 16),), jnp.float32)
    w_plus = normal_values(streams_of[4], (K, D), K ** -0.5, 1.25, ((1, 16),))
    w_minus = normal_values(streams_of[5], (K, D), K ** -0.5, 1.25, ((1, 16),))
    return dict(tokens=tokens, gain=gain, w_inputs=w_inputs, filters=filters, w_plus=w_plus, w_minus=w_minus)


EPS = 1e-05

def reference(tokens, gain, w_inputs, filters, w_plus, w_minus):
    values = tokens.astype(jnp.float32)
    power = lax.optimization_barrier(jnp.mean(values * values, axis=1, keepdims=True))
    scale = lax.rsqrt(power + EPS)
    scaled = (values * gain.astype(jnp.float32)).astype(jnp.bfloat16)
    projected = jnp.dot(scaled, w_inputs, preferred_element_type=jnp.float32) * scale
    lags = jnp.arange(SEQ, dtype=jnp.int32)
    lag_sign = 1.0 - 2.0 * (lags % 2).astype(jnp.float32)
    columns = filters.T
    response = jnp.dot(columns, w_plus.astype(jnp.float32), precision=lax.Precision.HIGHEST)
    response = response + lag_sign[:, None] * jnp.dot(columns, w_minus.astype(jnp.float32), precision=lax.Precision.HIGHEST)
    length = 2 * SEQ
    spectrum = jnp.fft.rfft(projected, n=length, axis=0) * jnp.fft.rfft(response, n=length, axis=0)
    mixed = jnp.fft.irfft(spectrum, n=length, axis=0)[:SEQ]
    return mixed.astype(jnp.bfloat16)
```

```python
import math

import jax
import jax.numpy as jnp
import ml_dtypes
import numpy as np
from jax import lax
from jax.experimental import pallas as pl
from jax.experimental.pallas import tpu as pltpu
from jax.sharding import PartitionSpec as P

EPS = 1e-05
HIGHEST = lax.Precision.HIGHEST
CTX, HI, YS, CORES = 16, 2, 4, 2
LANES = 128
FEATURES = 2048
SHARE = 8
ROWS = 1024
HALF = ROWS // CORES
BLOCKS = ROWS // LANES
PAD = 16
BF16, F32 = jnp.bfloat16, jnp.float32


def split_high_low(table):
    high = table.astype(ml_dtypes.bfloat16)
    low = (table - high.astype(np.float64)).astype(ml_dtypes.bfloat16)
    return high, low


def tables():
    ids = np.arange(LANES)
    quarter = ids + 0.25
    outer = np.exp(-2j * np.pi * np.outer(quarter, ids) / LANES)
    first = np.concatenate([outer.real, outer.imag], axis=0)
    twiddle = np.exp(-2j * np.pi * np.outer(quarter, ids) / LANES**2)
    inner = np.exp(-2j * np.pi * np.outer(ids, ids) / LANES)
    second = np.block([[inner.real, inner.imag], [-inner.imag, inner.real]])
    other = (ids // BLOCKS) * BLOCKS + (ids % BLOCKS + BLOCKS // 2) % BLOCKS
    natural = np.concatenate(split_high_low(first), axis=1)
    swapped = np.concatenate(split_high_low(first[:, other]), axis=1)
    last = split_high_low(first.T / LANES**2)
    return dict(
        first=np.stack([natural, swapped]),
        turn=np.stack([twiddle.real, twiddle.imag]).astype(np.float32),
        second=np.stack(split_high_low(second)),
        second_back=np.stack(split_high_low(second.T)),
        last=np.stack(last),
    )


def mm(left, right):
    return jnp.dot(left, right, preferred_element_type=F32)


def high_low(value):
    high = value.astype(BF16)
    return high, (value - high.astype(F32)).astype(BF16)


def mm3_right(value, table):
    high, low = high_low(value)
    return mm(high, table[0]) + mm(low, table[0]) + mm(high, table[1])


def mm3_left(table, value):
    high, low = high_low(value)
    return mm(table[0], high) + mm(table[0], low) + mm(table[1], high)


def spectrum_of_pair(pair, first, turn_real, turn_imag, second):
    mixed = mm(first, jnp.concatenate([pair, pair], axis=0))
    rows = []
    for at in range(2):
        real = mixed[:LANES, at * LANES : (at + 1) * LANES]
        imag = mixed[LANES:, at * LANES : (at + 1) * LANES]
        rows.append(
            jnp.concatenate(
                [real * turn_real - imag * turn_imag, real * turn_imag + imag * turn_real], axis=1
            )
        )
    return mm3_right(jnp.concatenate(rows, axis=0), second)


def load_pair(unpacked, at):
    return jnp.concatenate(
        [unpacked[pl.ds(2 * at + k, LANES, stride=SHARE), :] for k in range(2)], axis=1
    ).astype(BF16)


def filter_kernel(blocks_ref, first_ref, turn_ref, second_ref, out_ref, unpacked):
    unpacked[...] = blocks_ref[...].astype(F32).reshape(CTX * BLOCKS * SHARE, LANES)
    for at in range(SHARE // 2):
        out_ref[pl.ds(at * 2 * LANES, 2 * LANES), :] = spectrum_of_pair(
            load_pair(unpacked, at), first_ref[...], turn_ref[0], turn_ref[1], second_ref
        )


def mix_kernel(
    own_ref, other_ref, response_ref, first_ref, turn_ref, second_ref, back_ref, last_ref,
    out_ref, unpacked, gathered,
):
    half = BLOCKS * SHARE // 2
    both = jnp.concatenate([own_ref[:, :half, :], other_ref[...]], axis=1)
    unpacked[...] = both.astype(F32).reshape(CTX * BLOCKS * SHARE, LANES)
    turn_real, turn_imag = turn_ref[0], turn_ref[1]
    for at in range(SHARE // 2):
        signal = spectrum_of_pair(
            load_pair(unpacked, at), first_ref[...], turn_real, turn_imag, second_ref
        )
        response = response_ref[pl.ds(at * 2 * LANES, 2 * LANES), :]
        sig_real, sig_imag = signal[:, :LANES], signal[:, LANES:]
        res_real, res_imag = response[:, :LANES], response[:, LANES:]
        product = jnp.concatenate(
            [sig_real * res_real - sig_imag * res_imag, sig_real * res_imag + sig_imag * res_real],
            axis=1,
        )
        back = mm3_right(product, back_ref)
        reals, imags = [], []
        for k in range(2):
            real = back[k * LANES : (k + 1) * LANES, :LANES]
            imag = back[k * LANES : (k + 1) * LANES, LANES:]
            reals.append(real * turn_real + imag * turn_imag)
            imags.append(imag * turn_real - real * turn_imag)
        turned = jnp.concatenate(
            [jnp.concatenate(reals, axis=1), jnp.concatenate(imags, axis=1)], axis=0
        )
        result = mm3_left(last_ref, turned)
        for k in range(2):
            gathered[pl.ds(2 * at + k, LANES, stride=SHARE), :] = result[
                :, k * LANES : (k + 1) * LANES
            ]
    out_ref[...] = gathered[...].reshape(CTX, BLOCKS * SHARE, LANES).astype(BF16)


def project_kernel(
    place_ref, own_ref, left_ref, right_ref, mid_a_ref, mid_b_ref,
    far_ref, far_left_ref, far_right_ref, far_mid_a_ref, far_mid_b_ref,
    w_own_ref, w_other_ref, out_ref,
):
    high, along, core = place_ref[0], place_ref[1], place_ref[2]
    pieces = [
        (0, 0, own_ref, 0, own_ref, 1),
        (0, YS - 1, left_ref, 0, left_ref, 1),
        (0, 1, right_ref, 0, right_ref, 1),
        (0, 2, mid_a_ref, 0, mid_b_ref, 0),
        (1, 0, far_ref, 0, far_ref, 1),
        (1, YS - 1, far_left_ref, 0, far_left_ref, 1),
        (1, 1, far_right_ref, 0, far_right_ref, 1),
        (1, 2, far_mid_a_ref, 0, far_mid_b_ref, 0),
    ]
    total = jnp.zeros((HALF, 2 * LANES), F32)
    squares = jnp.zeros((HALF, LANES), F32)
    for d_high, d_along, ref_a, at_a, ref_b, at_b in pieces:
        chip = lax.rem(high + d_high, HI) * YS + lax.rem(along + d_along, YS)
        scaled, weights = [], []
        for slot, (ref, at) in enumerate(((ref_a, at_a), (ref_b, at_b))):
            values = ref[at, :HALF, :].astype(F32)
            squares = squares + values * values
            gain = ref[at, HALF : HALF + PAD, :].astype(F32)[:1]
            scaled.append((values * gain).astype(BF16))
            owner = chip * CORES + (core if slot == 0 else 1 - core)
            start = pl.multiple_of(owner * LANES, LANES)
            weights.append(
                jnp.concatenate(
                    [w_own_ref[pl.ds(start, LANES), :], w_other_ref[pl.ds(start, LANES), :]],
                    axis=1,
                )
            )
        total = total + mm(jnp.concatenate(scaled, axis=1), jnp.concatenate(weights, axis=0))
    power = jnp.sum(squares, axis=1, keepdims=True) * (1.0 / FEATURES)
    total = total * lax.rsqrt(power + EPS)
    for slot in range(CORES):
        for pair in range(BLOCKS // CORES // 2):
            parts = []
            for k in range(2):
                block = 2 * pair + k
                part = total[
                    block * LANES : (block + 1) * LANES, slot * LANES : (slot + 1) * LANES
                ]
                parts.append(part.T.reshape(CTX, SHARE, LANES))
            start = slot * (BLOCKS * SHARE // 2) + pair * 2 * SHARE
            out_ref[:, start : start + 2 * SHARE, :] = jnp.concatenate(parts, axis=1).astype(BF16)


def turn_kernel(blocks_ref, out_ref):
    for pair in range(BLOCKS // 2):
        values = blocks_ref[:, pair * 2 * SHARE : (pair + 1) * 2 * SHARE, :].astype(F32)
        for k in range(2):
            part = values[:, k * SHARE : (k + 1) * SHARE, :].reshape(LANES, LANES)
            start = (2 * pair + k) * LANES
            out_ref[start : start + LANES, :] = part.T.astype(BF16)


VMEM = pl.BlockSpec(memory_space=pltpu.VMEM)
SMEM = pl.BlockSpec(memory_space=pltpu.SMEM)
PARAMS = pltpu.CompilerParams(vmem_limit_bytes=48 * 1024 * 1024)


def call(kernel, shape, dtype, operands, scratch=(), first_spec=VMEM, flops=0):
    moved = sum(x.size * x.dtype.itemsize for x in operands)
    return pl.pallas_call(
        kernel,
        out_shape=jax.ShapeDtypeStruct(shape, dtype),
        in_specs=[first_spec] + [VMEM] * (len(operands) - 1),
        out_specs=VMEM,
        scratch_shapes=list(scratch),
        compiler_params=PARAMS,
        cost_estimate=pl.CostEstimate(flops=flops, bytes_accessed=moved, transcendentals=0),
    )(*operands)


def tp_shift(value, d_high, d_along, d_core):
    pairs = []
    for high in range(HI):
        for along in range(YS):
            for core in range(CORES):
                source = (high * YS + along) * CORES + core
                target = (
                    (high + d_high) % HI * YS + (along + d_along) % YS
                ) * CORES + (core + d_core) % CORES
                pairs.append((source, target))
    return lax.ppermute(value, "tp", pairs)


def rings(piece):
    left = tp_shift(piece, 0, 1, 0)
    right = tp_shift(piece, 0, YS - 1, 0)
    mid_a = tp_shift(left[:1], 0, 1, 0)
    mid_b = tp_shift(right[1:], 0, YS - 1, 0)
    return left, right, mid_a, mid_b


def on_device(tokens, gain, w_inputs, filters, w_plus, w_minus):
    table = tables()
    position = lax.axis_index("tp")
    core = lax.rem(position, CORES)
    place = jnp.stack(
        [position // (YS * CORES), lax.rem(position // CORES, YS), core, core]
    ).astype(jnp.int32)

    gain_rows = jnp.broadcast_to(gain[None, :], (PAD, LANES))
    mine = lax.dynamic_slice_in_dim(tokens, core * HALF, HALF, axis=0)
    theirs = lax.dynamic_slice_in_dim(tokens, (1 - core) * HALF, HALF, axis=0)
    arrived = tp_shift(jnp.concatenate([theirs, gain_rows], axis=0), 0, 0, 1)
    own = jnp.stack([jnp.concatenate([mine, gain_rows], axis=0), arrived])
    far = tp_shift(own, 1, 0, 0)
    near_parts = rings(own)
    far_parts = rings(far)
    w_other = tp_shift(w_inputs, 0, 0, 1)

    lag_sign = 1.0 - 2.0 * (lax.iota(jnp.int32, ROWS) % 2).astype(F32)
    response = jnp.einsum("kt,kc->ct", filters, w_plus.astype(F32), precision=HIGHEST)
    response = response + lag_sign[None, :] * jnp.einsum(
        "kt,kc->ct", filters, w_minus.astype(F32), precision=HIGHEST
    )
    response = (
        response.reshape(CTX, SHARE, BLOCKS, LANES)
        .transpose(0, 2, 1, 3)
        .astype(BF16)
        .reshape(CTX, BLOCKS * SHARE, LANES)
    )
    response = lax.all_to_all(response, "ctx", split_axis=0, concat_axis=0, tiled=True)
    unpacked = pltpu.VMEM((CTX * BLOCKS * SHARE, LANES), F32)
    turn, second = jnp.asarray(table["turn"]), jnp.asarray(table["second"])
    first = jnp.asarray(table["first"])
    response = call(
        filter_kernel,
        (SHARE * LANES, 2 * LANES),
        F32,
        [response, first[0], turn, second],
        [unpacked],
        flops=10**9,
    )

    operands = [place, own, *near_parts, far, *far_parts, w_inputs, w_other]
    blocks = call(
        project_kernel,
        (CTX, BLOCKS * SHARE, LANES),
        BF16,
        operands,
        first_spec=SMEM,
        flops=2 * HALF * 2 * LANES * FEATURES,
    )
    blocks = lax.all_to_all(blocks, "ctx", split_axis=0, concat_axis=0, tiled=True)
    other = tp_shift(blocks[:, BLOCKS * SHARE // 2 :, :], 0, 0, 1)
    mixed = call(
        mix_kernel,
        (CTX, BLOCKS * SHARE, LANES),
        BF16,
        [
            blocks,
            other,
            response,
            lax.dynamic_index_in_dim(first, core, axis=0, keepdims=False),
            turn,
            second,
            jnp.asarray(table["second_back"]),
            jnp.asarray(table["last"]),
        ],
        [unpacked, unpacked],
        flops=2 * 10**9,
    )
    mixed = lax.all_to_all(mixed, "ctx", split_axis=0, concat_axis=0, tiled=True)
    return call(turn_kernel, (ROWS, LANES), BF16, [mixed])


def solution(mesh):
    in_specs = (
        P("ctx", "tp"),
        P("tp"),
        P(None, "tp"),
        P(None, "ctx"),
        P(None, "tp"),
        P(None, "tp"),
    )
    return jax.shard_map(
        on_device, mesh=mesh, in_specs=in_specs, out_specs=P("ctx", "tp"), check_vma=False
    )
```

```python
import functools
import math

import jax
import jax.numpy as jnp
import ml_dtypes
import numpy as np
from jax import lax
from jax.experimental import pallas as pl
from jax.experimental.pallas import tpu as pltpu
from jax.sharding import PartitionSpec as P

EPS = 1e-05
HIGHEST = lax.Precision.HIGHEST
CTX, HI, YS, CORES = 16, 2, 4, 2
LANES = 128
FEATURES = 2048
SHARE = 8
ROWS = 1024
HALF = ROWS // CORES
BLOCKS = ROWS // LANES
PAD = 16
BF16, F32 = jnp.bfloat16, jnp.float32


def split_high_low(table):
    high = table.astype(ml_dtypes.bfloat16)
    low = (table - high.astype(np.float64)).astype(ml_dtypes.bfloat16)
    return high, low


def tables():
    ids = np.arange(LANES)
    quarter = ids + 0.25
    outer = np.exp(-2j * np.pi * np.outer(quarter, ids) / LANES)
    first = np.concatenate([outer.real, outer.imag], axis=0)
    twiddle = np.exp(-2j * np.pi * np.outer(quarter, ids) / LANES**2)
    inner = np.exp(-2j * np.pi * np.outer(ids, ids) / LANES)
    second = np.block([[inner.real, inner.imag], [-inner.imag, inner.real]])
    other = (ids // BLOCKS) * BLOCKS + (ids % BLOCKS + BLOCKS // 2) % BLOCKS
    natural = np.concatenate(split_high_low(first), axis=1)
    swapped = np.concatenate(split_high_low(first[:, other]), axis=1)
    last = split_high_low(first.T / LANES**2)
    return dict(
        first=np.stack([natural, swapped]),
        turn=np.stack([twiddle.real, twiddle.imag]).astype(np.float32),
        second=np.stack(split_high_low(second)),
        second_back=np.stack(split_high_low(second.T)),
        last=np.stack(last),
    )


def mm(left, right):
    return jnp.dot(left, right, preferred_element_type=F32)


def high_low(value):
    high = value.astype(BF16)
    return high, (value - high.astype(F32)).astype(BF16)


def mm3_right(value, table):
    high, low = high_low(value)
    return mm(high, table[0]) + mm(low, table[0]) + mm(high, table[1])


def mm3_left(table, value):
    high, low = high_low(value)
    return mm(table[0], high) + mm(table[0], low) + mm(table[1], high)


def spectrum_of_pair(pair, first, turn_real, turn_imag, second):
    mixed = mm(first, jnp.concatenate([pair, pair], axis=0))
    rows = []
    for at in range(2):
        real = mixed[:LANES, at * LANES : (at + 1) * LANES]
        imag = mixed[LANES:, at * LANES : (at + 1) * LANES]
        rows.append(
            jnp.concatenate(
                [real * turn_real - imag * turn_imag, real * turn_imag + imag * turn_real], axis=1
            )
        )
    return mm3_right(jnp.concatenate(rows, axis=0), second)


def load_pair(unpacked, at):
    return jnp.concatenate(
        [unpacked[pl.ds(2 * at + k, LANES, stride=SHARE), :] for k in range(2)], axis=1
    ).astype(BF16)


def unpack(ref, values):
    ref[...] = values.astype(F32).reshape(CTX * BLOCKS * SHARE, LANES)


def mix_kernel(
    place_ref, own_ref, other_ref, first_ref, turn_ref, second_ref, back_ref, last_ref,
    out_ref, signals, responses, gathered,
):
    full = BLOCKS * SHARE
    half = full // 2
    unpack(signals, jnp.concatenate([own_ref[:, :half, :], other_ref[...]], axis=1))
    unpack(responses, own_ref[:, full:, :])
    turn_real, turn_imag = turn_ref[0], turn_ref[1]
    first_here = first_ref[place_ref[2]]
    first = first_ref[0]
    for at in range(SHARE // 2):
        signal = spectrum_of_pair(
            load_pair(signals, at), first_here, turn_real, turn_imag, second_ref
        )
        response = spectrum_of_pair(
            load_pair(responses, at), first, turn_real, turn_imag, second_ref
        )
        sig_real, sig_imag = signal[:, :LANES], signal[:, LANES:]
        res_real, res_imag = response[:, :LANES], response[:, LANES:]
        product = jnp.concatenate(
            [sig_real * res_real - sig_imag * res_imag, sig_real * res_imag + sig_imag * res_real],
            axis=1,
        )
        back = mm3_right(product, back_ref)
        reals, imags = [], []
        for k in range(2):
            real = back[k * LANES : (k + 1) * LANES, :LANES]
            imag = back[k * LANES : (k + 1) * LANES, LANES:]
            reals.append(real * turn_real + imag * turn_imag)
            imags.append(imag * turn_real - real * turn_imag)
        turned = jnp.concatenate(
            [jnp.concatenate(reals, axis=1), jnp.concatenate(imags, axis=1)], axis=0
        )
        result = mm3_left(last_ref, turned)
        for k in range(2):
            gathered[pl.ds(2 * at + k, LANES, stride=SHARE), :] = result[
                :, k * LANES : (k + 1) * LANES
            ]
    out_ref[...] = gathered[...].reshape(CTX, full, LANES).astype(BF16)


def project_kernel(pieces, place_ref, *refs):
    high, along, core = place_ref[0], place_ref[1], place_ref[2]
    *piece_refs, w_own_ref, w_other_ref, response_ref, out_ref = refs
    count = HALF // LANES
    total = jnp.zeros((HALF, 2 * LANES), F32)
    squares = jnp.zeros((HALF, LANES), F32)
    for d_high, d_along, *slots in pieces:
        chip = lax.rem(high + d_high, HI) * YS + lax.rem(along + d_along, YS)
        scaled, weights = [], []
        for slot, (at, lead) in enumerate(slots):
            ref = piece_refs[at]
            block = ref[...] if lead is None else ref[lead]
            values = block[:HALF].astype(F32)
            squares = squares + values * values
            scaled.append((values * block[HALF:].astype(F32)[:1]).astype(BF16))
            owner = chip * CORES + (core if slot == 0 else 1 - core)
            start = pl.multiple_of(owner * LANES, LANES)
            weights.append(
                jnp.concatenate(
                    [w_own_ref[pl.ds(start, LANES), :], w_other_ref[pl.ds(start, LANES), :]],
                    axis=1,
                )
            )
        total = total + mm(jnp.concatenate(scaled, axis=1), jnp.concatenate(weights, axis=0))
    power = jnp.sum(squares, axis=1, keepdims=True) * (1.0 / FEATURES)
    total = total * lax.rsqrt(power + EPS)
    for slot in range(CORES):
        for pair in range(count // 2):
            parts = []
            for block in (2 * pair, 2 * pair + 1):
                part = total[
                    block * LANES : (block + 1) * LANES, slot * LANES : (slot + 1) * LANES
                ]
                parts.append(part.T.reshape(CTX, SHARE, LANES))
            start = (slot * count + 2 * pair) * SHARE
            out_ref[:, start : start + 2 * SHARE, :] = jnp.concatenate(parts, axis=1).astype(BF16)
    out_ref[:, BLOCKS * SHARE :, :] = response_ref[...]


def turn_kernel(blocks_ref, out_ref):
    for pair in range(BLOCKS // 2):
        values = blocks_ref[:, pair * 2 * SHARE : (pair + 1) * 2 * SHARE, :].astype(F32)
        for k in range(2):
            part = values[:, k * SHARE : (k + 1) * SHARE, :].reshape(LANES, LANES)
            start = (2 * pair + k) * LANES
            out_ref[start : start + LANES, :] = part.T.astype(BF16)


VMEM = pl.BlockSpec(memory_space=pltpu.VMEM)
SMEM = pl.BlockSpec(memory_space=pltpu.SMEM)
PARAMS = pltpu.CompilerParams(vmem_limit_bytes=48 * 1024 * 1024)


def call(kernel, outs, operands, scratch=(), first_spec=VMEM, flops=0):
    moved = sum(x.size * x.dtype.itemsize for x in operands)
    return pl.pallas_call(
        kernel,
        out_shape=outs,
        in_specs=[first_spec] + [VMEM] * (len(operands) - 1),
        out_specs=jax.tree.map(lambda _: VMEM, outs),
        scratch_shapes=list(scratch),
        compiler_params=PARAMS,
        cost_estimate=pl.CostEstimate(flops=flops, bytes_accessed=moved, transcendentals=0),
    )(*operands)


def bf16(*shape):
    return jax.ShapeDtypeStruct(shape, BF16)


def tp_shift(value, d_high, d_along, d_core):
    pairs = []
    for high in range(HI):
        for along in range(YS):
            for core in range(CORES):
                source = (high * YS + along) * CORES + core
                target = (
                    (high + d_high) % HI * YS + (along + d_along) % YS
                ) * CORES + (core + d_core) % CORES
                pairs.append((source, target))
    return lax.ppermute(value, "tp", pairs)


AG = "G6"


def gather(mine, theirs):
    def left(x, swap=0):
        return tp_shift(x, 0, 1, swap)

    def right(x, swap=0):
        return tp_shift(x, 0, YS - 1, swap)

    arrived = tp_shift(theirs, 0, 0, 1)
    out, pieces = [], []

    def add(d_high, d_along, *slots):
        entry = [d_high, d_along]
        for value, lead in slots:
            for at, known in enumerate(out):
                if known is value:
                    break
            else:
                at = len(out)
                out.append(value)
            entry.append((at, lead))
        pieces.append(tuple(entry))

    def add_whole(d_high, d_along, value):
        add(d_high, d_along, (value, 0), (value, 1))

    def ring_whole(d_high, value):
        l, r = left(value), right(value)
        ma, mb = left(l[0]), right(r[1])
        add_whole(d_high, 0, value)
        add_whole(d_high, YS - 1, l)
        add_whole(d_high, 1, r)
        add(d_high, 2, (ma, None), (mb, None))

    def ring_slots(d_high, a, b, src=None, swap=0):
        src = b if src is None else src
        la, rb = left(a), right(src, swap)
        ra, lb = right(a), left(src, swap)
        ma, mb = left(la), right(rb)
        add(d_high, 0, (a, None), (b, None))
        add(d_high, YS - 1, (la, None), (lb, None))
        add(d_high, 1, (ra, None), (rb, None))
        add(d_high, 2, (ma, None), (mb, None))

    own = jnp.stack([mine, arrived])
    if AG == "G1":
        far = tp_shift(own, 1, 0, 0)
        ring_whole(0, own)
        ring_whole(1, far)
    elif AG == "G2":
        za, zb = tp_shift(mine, 1, 0, 0), tp_shift(arrived, 1, 0, 0)
        ring_whole(0, own)
        ring_slots(1, za, zb)
    elif AG == "G3":
        za, zb = tp_shift(mine, 1, 0, 0), tp_shift(arrived, 1, 0, 0)
        ring_slots(0, mine, arrived)
        ring_slots(1, za, zb)
    elif AG == "G4":
        za, zb = tp_shift(mine, 1, 0, 0), tp_shift(theirs, 1, 0, 1)
        ring_slots(0, mine, arrived, theirs, 1)
        ring_slots(1, za, zb)
    elif AG == "G5":
        za, zb = tp_shift(mine, 1, 0, 0), tp_shift(theirs, 1, 0, 1)
        ring_whole(0, own)
        ring_slots(1, za, zb)
    elif AG == "G6":
        za, zb = tp_shift(mine, 1, 0, 0), tp_shift(theirs, 1, 0, 1)
        far = jnp.stack([za, zb])
        ring_whole(0, own)
        ring_whole(1, far)
    return out, tuple(pieces)


def on_device(tokens, gain, w_inputs, filters, w_plus, w_minus):
    table = tables()
    position = lax.axis_index("tp")
    core = lax.rem(position, CORES)
    place = jnp.stack(
        [position // (YS * CORES), lax.rem(position // CORES, YS), core, core]
    ).astype(jnp.int32)

    gain_rows = jnp.broadcast_to(gain[None, :], (PAD, LANES))
    mine, theirs = (
        jnp.concatenate(
            [lax.dynamic_slice_in_dim(tokens, half * HALF, HALF, axis=0), gain_rows], axis=0
        )
        for half in (core, 1 - core)
    )
    gathered, pieces = gather(mine, theirs)
    w_other = tp_shift(w_inputs, 0, 0, 1)

    lag_sign = 1.0 - 2.0 * (lax.iota(jnp.int32, ROWS) % 2).astype(F32)
    response = jnp.einsum("kt,kc->ct", filters, w_plus.astype(F32), precision=HIGHEST)
    response = response + lag_sign[None, :] * jnp.einsum(
        "kt,kc->ct", filters, w_minus.astype(F32), precision=HIGHEST
    )
    response = (
        response.reshape(CTX, SHARE, BLOCKS, LANES)
        .transpose(0, 2, 1, 3)
        .astype(BF16)
        .reshape(CTX, BLOCKS * SHARE, LANES)
    )

    blocks = call(
        functools.partial(project_kernel, pieces),
        bf16(CTX, 2 * BLOCKS * SHARE, LANES),
        [place, *gathered, w_inputs, w_other, response],
        first_spec=SMEM,
        flops=2 * HALF * 2 * LANES * FEATURES,
    )
    blocks = lax.all_to_all(blocks, "ctx", split_axis=0, concat_axis=0, tiled=True)
    other = tp_shift(blocks[:, BLOCKS * SHARE // 2 : BLOCKS * SHARE, :], 0, 0, 1)
    consts = [jnp.asarray(table[k]) for k in ("first", "turn", "second", "second_back", "last")]
    unpacked = pltpu.VMEM((CTX * BLOCKS * SHARE, LANES), F32)
    mixed = call(
        mix_kernel,
        bf16(CTX, BLOCKS * SHARE, LANES),
        [place, blocks, other, *consts],
        [unpacked, unpacked, unpacked],
        first_spec=SMEM,
        flops=3 * 10**9,
    )
    mixed = lax.all_to_all(mixed, "ctx", split_axis=0, concat_axis=0, tiled=True)
    return call(turn_kernel, bf16(ROWS, LANES), [mixed])


def solution(mesh):
    in_specs = (
        P("ctx", "tp"),
        P("tp"),
        P(None, "tp"),
        P(None, "ctx"),
        P(None, "tp"),
        P(None, "tp"),
    )
    return jax.shard_map(
        on_device, mesh=mesh, in_specs=in_specs, out_specs=P("ctx", "tp"), check_vma=False
    )
```

```python
import math

import jax
import jax.numpy as jnp
import ml_dtypes
import numpy as np
from jax import lax
from jax.experimental import pallas as pl
from jax.experimental.pallas import tpu as pltpu
from jax.sharding import PartitionSpec as P

EPS = 1e-05
HIGHEST = lax.Precision.HIGHEST
CTX, HI, YS, CORES = 16, 2, 4, 2
LANES = 128
FEATURES = 2048
SHARE = 8
ROWS = 1024
HALF = ROWS // CORES
BLOCKS = ROWS // LANES
PAD = 16
BF16, F32 = jnp.bfloat16, jnp.float32


def split_high_low(table):
    high = table.astype(ml_dtypes.bfloat16)
    low = (table - high.astype(np.float64)).astype(ml_dtypes.bfloat16)
    return high, low


def tables():
    ids = np.arange(LANES)
    quarter = ids + 0.25
    outer = np.exp(-2j * np.pi * np.outer(quarter, ids) / LANES)
    first = np.concatenate([outer.real, outer.imag], axis=0)
    twiddle = np.exp(-2j * np.pi * np.outer(quarter, ids) / LANES**2)
    inner = np.exp(-2j * np.pi * np.outer(ids, ids) / LANES)
    second = np.block([[inner.real, inner.imag], [-inner.imag, inner.real]])
    other = (ids // BLOCKS) * BLOCKS + (ids % BLOCKS + BLOCKS // 2) % BLOCKS
    natural = np.concatenate(split_high_low(first), axis=1)
    swapped = np.concatenate(split_high_low(first[:, other]), axis=1)
    last = split_high_low(first.T / LANES**2)
    return dict(
        first=np.stack([natural, swapped]),
        turn=np.stack([twiddle.real, twiddle.imag]).astype(np.float32),
        second=np.stack(split_high_low(second)),
        second_back=np.stack(split_high_low(second.T)),
        last=np.stack(last),
    )


def mm(left, right):
    return jnp.dot(left, right, preferred_element_type=F32)


def high_low(value):
    high = value.astype(BF16)
    return high, (value - high.astype(F32)).astype(BF16)


def mm3_right(value, table):
    high, low = high_low(value)
    return mm(
        jnp.concatenate([high, low, high], axis=1),
        jnp.concatenate([table[0], table[0], table[1]], axis=0),
    )


def mm3_left(table, value):
    high, low = high_low(value)
    return mm(
        jnp.concatenate([table[0], table[0], table[1]], axis=1),
        jnp.concatenate([high, low, high], axis=0),
    )


def turned_blocks(values, first, turn_real, turn_imag):
    mixed = mm(first, jnp.concatenate([values, values], axis=0))
    rows = []
    for at in range(SHARE):
        real = mixed[:LANES, at * LANES : (at + 1) * LANES]
        imag = mixed[LANES:, at * LANES : (at + 1) * LANES]
        rows.append(
            jnp.concatenate(
                [real * turn_real - imag * turn_imag, real * turn_imag + imag * turn_real], axis=1
            )
        )
    return jnp.concatenate(rows, axis=0)


def load_all(unpacked, values):
    unpacked[...] = values.astype(F32).reshape(CTX * BLOCKS * SHARE, LANES)
    return jnp.concatenate(
        [unpacked[pl.ds(at, LANES, stride=SHARE), :] for at in range(SHARE)], axis=1
    ).astype(BF16)


def mix_kernel(
    place_ref, own_ref, other_ref, first_ref, turn_ref, second_ref, back_ref, last_ref,
    out_ref, signals, responses, gathered,
):
    full = BLOCKS * SHARE
    turn_real, turn_imag = turn_ref[0], turn_ref[1]
    first = first_ref[0]
    signal = load_all(
        signals, jnp.concatenate([own_ref[:, : full // 2, :], other_ref[...]], axis=1)
    )
    response = load_all(responses, own_ref[:, full:, :])
    signal = turned_blocks(signal, first_ref[place_ref[2]], turn_real, turn_imag)
    signal = mm3_right(signal, second_ref)
    response = mm3_right(turned_blocks(response, first, turn_real, turn_imag), second_ref)
    sig_real, sig_imag = signal[:, :LANES], signal[:, LANES:]
    res_real, res_imag = response[:, :LANES], response[:, LANES:]
    product = jnp.concatenate(
        [sig_real * res_real - sig_imag * res_imag, sig_real * res_imag + sig_imag * res_real],
        axis=1,
    )
    back = mm3_right(product, back_ref)
    reals, imags = [], []
    for at in range(SHARE):
        real = back[at * LANES : (at + 1) * LANES, :LANES]
        imag = back[at * LANES : (at + 1) * LANES, LANES:]
        reals.append(real * turn_real + imag * turn_imag)
        imags.append(imag * turn_real - real * turn_imag)
    turned = jnp.concatenate(
        [jnp.concatenate(reals, axis=1), jnp.concatenate(imags, axis=1)], axis=0
    )
    result = mm3_left(last_ref, turned)
    for at in range(SHARE):
        gathered[pl.ds(at, LANES, stride=SHARE), :] = result[:, at * LANES : (at + 1) * LANES]
    out_ref[...] = gathered[...].reshape(CTX, BLOCKS * SHARE, LANES).astype(BF16)


def add_products(d_high, place_ref, piece_refs, w_own_ref, w_other_ref, total, squares):
    high, along, core = place_ref[0], place_ref[1], place_ref[2]
    whole_refs, mid_refs = piece_refs[:3], piece_refs[3:]
    for d_along, ref in (*zip((0, YS - 1, 1), whole_refs), (2, None)):
        chip = lax.rem(high + d_high, HI) * YS + lax.rem(along + d_along, YS)
        scaled, weights = [], []
        for slot in range(CORES):
            block = mid_refs[slot][...] if ref is None else ref[slot]
            values = block[:HALF].astype(F32)
            squares = squares + values * values
            scaled.append((values * block[HALF:].astype(F32)[:1]).astype(BF16))
            owner = chip * CORES + (core if slot == 0 else 1 - core)
            start = pl.multiple_of(owner * LANES, LANES)
            weights.append(
                jnp.concatenate(
                    [w_own_ref[pl.ds(start, LANES), :], w_other_ref[pl.ds(start, LANES), :]],
                    axis=1,
                )
            )
        total = total + mm(jnp.concatenate(scaled, axis=1), jnp.concatenate(weights, axis=0))
    return total, squares


def near_kernel(place_ref, *refs):
    *piece_refs, w_own_ref, w_other_ref, total_ref, squares_ref = refs
    total_ref[...], squares_ref[...] = add_products(
        0,
        place_ref,
        piece_refs,
        w_own_ref,
        w_other_ref,
        jnp.zeros((HALF, 2 * LANES), F32),
        jnp.zeros((HALF, LANES), F32),
    )


def project_kernel(place_ref, *refs):
    *piece_refs, w_own_ref, w_other_ref, response_ref, total_ref, squares_ref, out_ref = refs
    count = HALF // LANES
    total, squares = add_products(
        1, place_ref, piece_refs, w_own_ref, w_other_ref, total_ref[...], squares_ref[...]
    )
    power = jnp.sum(squares, axis=1, keepdims=True) * (1.0 / FEATURES)
    total = total * lax.rsqrt(power + EPS)
    for slot in range(CORES):
        for pair in range(count // 2):
            parts = []
            for block in (2 * pair, 2 * pair + 1):
                part = total[
                    block * LANES : (block + 1) * LANES, slot * LANES : (slot + 1) * LANES
                ]
                parts.append(part.T.reshape(CTX, SHARE, LANES))
            start = (slot * count + 2 * pair) * SHARE
            out_ref[:, start : start + 2 * SHARE, :] = jnp.concatenate(parts, axis=1).astype(BF16)
    out_ref[:, BLOCKS * SHARE :, :] = response_ref[...]


def turn_kernel(blocks_ref, out_ref):
    for pair in range(BLOCKS // 2):
        values = blocks_ref[:, pair * 2 * SHARE : (pair + 1) * 2 * SHARE, :].astype(F32)
        for k in range(2):
            part = values[:, k * SHARE : (k + 1) * SHARE, :].reshape(LANES, LANES)
            start = (2 * pair + k) * LANES
            out_ref[start : start + LANES, :] = part.T.astype(BF16)


VMEM = pl.BlockSpec(memory_space=pltpu.VMEM)
SMEM = pl.BlockSpec(memory_space=pltpu.SMEM)
PARAMS = pltpu.CompilerParams(vmem_limit_bytes=48 * 1024 * 1024)


def call(kernel, outs, operands, scratch=(), first_spec=VMEM, flops=0):
    moved = sum(x.size * x.dtype.itemsize for x in operands)
    return pl.pallas_call(
        kernel,
        out_shape=outs,
        in_specs=[first_spec] + [VMEM] * (len(operands) - 1),
        out_specs=jax.tree.map(lambda _: VMEM, outs),
        scratch_shapes=list(scratch),
        compiler_params=PARAMS,
        cost_estimate=pl.CostEstimate(flops=flops, bytes_accessed=moved, transcendentals=0),
    )(*operands)


def bf16(*shape):
    return jax.ShapeDtypeStruct(shape, BF16)


def tp_shift(value, d_high, d_along, d_core):
    pairs = []
    for high in range(HI):
        for along in range(YS):
            for core in range(CORES):
                source = (high * YS + along) * CORES + core
                target = (
                    (high + d_high) % HI * YS + (along + d_along) % YS
                ) * CORES + (core + d_core) % CORES
                pairs.append((source, target))
    return lax.ppermute(value, "tp", pairs)


def gather(mine, theirs):
    def left(value):
        return tp_shift(value, 0, 1, 0)

    def right(value):
        return tp_shift(value, 0, YS - 1, 0)

    def ring(value):
        from_left, from_right = left(value), right(value)
        return [value, from_left, from_right, left(from_left[0]), right(from_right[1])]

    across = [tp_shift(mine, 1, 0, 0), tp_shift(theirs, 1, 0, 1)]
    own = jnp.stack([mine, tp_shift(theirs, 0, 0, 1)])
    return ring(own), ring(jnp.stack(across))


def on_device(tokens, gain, w_inputs, filters, w_plus, w_minus):
    table = tables()
    position = lax.axis_index("tp")
    core = lax.rem(position, CORES)
    place = jnp.stack(
        [position // (YS * CORES), lax.rem(position // CORES, YS), core, core]
    ).astype(jnp.int32)

    gain_rows = jnp.broadcast_to(gain[None, :], (PAD, LANES))
    mine, theirs = (
        jnp.concatenate(
            [lax.dynamic_slice_in_dim(tokens, half * HALF, HALF, axis=0), gain_rows], axis=0
        )
        for half in (core, 1 - core)
    )
    near, far = gather(mine, theirs)
    w_other = tp_shift(w_inputs, 0, 0, 1)

    lag_sign = 1.0 - 2.0 * (lax.iota(jnp.int32, ROWS) % 2).astype(F32)
    response = jnp.einsum("kt,kc->ct", filters, w_plus.astype(F32), precision=HIGHEST)
    response = response + lag_sign[None, :] * jnp.einsum(
        "kt,kc->ct", filters, w_minus.astype(F32), precision=HIGHEST
    )
    response = (
        response.reshape(CTX, SHARE, BLOCKS, LANES)
        .transpose(0, 2, 1, 3)
        .astype(BF16)
        .reshape(CTX, BLOCKS * SHARE, LANES)
    )

    flops = HALF * 2 * LANES * FEATURES
    total, squares = call(
        near_kernel,
        (
            jax.ShapeDtypeStruct((HALF, 2 * LANES), F32),
            jax.ShapeDtypeStruct((HALF, LANES), F32),
        ),
        [place, *near, w_inputs, w_other],
        first_spec=SMEM,
        flops=flops,
    )
    blocks = call(
        project_kernel,
        bf16(CTX, 2 * BLOCKS * SHARE, LANES),
        [place, *far, w_inputs, w_other, response, total, squares],
        first_spec=SMEM,
        flops=flops,
    )
    blocks = lax.all_to_all(blocks, "ctx", split_axis=0, concat_axis=0, tiled=True)
    other = tp_shift(blocks[:, BLOCKS * SHARE // 2 : BLOCKS * SHARE, :], 0, 0, 1)
    consts = [jnp.asarray(table[k]) for k in ("first", "turn", "second", "second_back", "last")]
    unpacked = pltpu.VMEM((CTX * BLOCKS * SHARE, LANES), F32)
    mixed = call(
        mix_kernel,
        bf16(CTX, BLOCKS * SHARE, LANES),
        [place, blocks, other, *consts],
        [unpacked, unpacked, unpacked],
        first_spec=SMEM,
        flops=3 * 10**9,
    )
    mixed = lax.all_to_all(mixed, "ctx", split_axis=0, concat_axis=0, tiled=True)
    return call(turn_kernel, bf16(ROWS, LANES), [mixed])


def solution(mesh):
    in_specs = (
        P("ctx", "tp"),
        P("tp"),
        P(None, "tp"),
        P(None, "ctx"),
        P(None, "tp"),
        P(None, "tp"),
    )
    return jax.shard_map(
        on_device, mesh=mesh, in_specs=in_specs, out_specs=P("ctx", "tp"), check_vma=False
    )
```

```python
import math

import jax
import jax.numpy as jnp
import ml_dtypes
import numpy as np
from jax import lax
from jax.experimental import pallas as pl
from jax.experimental.pallas import tpu as pltpu
from jax.sharding import PartitionSpec as P

EPS = 1e-05
HIGHEST = lax.Precision.HIGHEST
CTX, HI, YS, CORES = 16, 2, 4, 2
LANES = 128
FEATURES = 2048
SHARE = 8
ROWS = 1024
HALF = ROWS // CORES
BLOCKS = ROWS // LANES
PAD = 16
BF16, F32 = jnp.bfloat16, jnp.float32


def split_high_low(table):
    high = table.astype(ml_dtypes.bfloat16)
    low = (table - high.astype(np.float64)).astype(ml_dtypes.bfloat16)
    return high, low


def tables():
    ids = np.arange(LANES)
    quarter = ids + 0.25
    outer = np.exp(-2j * np.pi * np.outer(quarter, ids) / LANES)
    first = np.concatenate([outer.real, outer.imag], axis=0)
    twiddle = np.exp(-2j * np.pi * np.outer(quarter, ids) / LANES**2)
    inner = np.exp(-2j * np.pi * np.outer(ids, ids) / LANES)
    second = np.block([[inner.real, inner.imag], [-inner.imag, inner.real]])
    other = (ids // BLOCKS) * BLOCKS + (ids % BLOCKS + BLOCKS // 2) % BLOCKS
    natural = np.concatenate(split_high_low(first), axis=1)
    swapped = np.concatenate(split_high_low(first[:, other]), axis=1)
    last = split_high_low(first.T / LANES**2)
    return dict(
        first=np.stack([natural, swapped]),
        turn=np.stack([twiddle.real, twiddle.imag]).astype(np.float32),
        second=np.stack(split_high_low(second)),
        second_back=np.stack(split_high_low(second.T)),
        last=np.stack(last),
    )


def mm(left, right):
    return jnp.dot(left, right, preferred_element_type=F32)


def high_low(value):
    high = value.astype(BF16)
    return high, (value - high.astype(F32)).astype(BF16)


def mm3_right(value, table):
    high, low = high_low(value)
    return mm(
        jnp.concatenate([high, low, high], axis=1),
        jnp.concatenate([table[0], table[0], table[1]], axis=0),
    )


def mm3_left(table, value):
    high, low = high_low(value)
    return mm(
        jnp.concatenate([table[0], table[0], table[1]], axis=1),
        jnp.concatenate([high, low, high], axis=0),
    )


def turned_blocks(values, first, turn_real, turn_imag):
    mixed = mm(first, jnp.concatenate([values, values], axis=0))
    rows = []
    for at in range(SHARE):
        real = mixed[:LANES, at * LANES : (at + 1) * LANES]
        imag = mixed[LANES:, at * LANES : (at + 1) * LANES]
        rows.append(
            jnp.concatenate(
                [real * turn_real - imag * turn_imag, real * turn_imag + imag * turn_real], axis=1
            )
        )
    return jnp.concatenate(rows, axis=0)


def load_all(unpacked, values):
    unpacked[: CTX * BLOCKS * SHARE, :] = values.astype(F32).reshape(CTX * BLOCKS * SHARE, LANES)
    return jnp.concatenate(
        [unpacked[pl.ds(at, LANES, stride=SHARE), :] for at in range(SHARE)], axis=1
    ).astype(BF16)


def mix_kernel(
    place_ref, own_ref, other_ref, first_ref, turn_ref, second_ref, back_ref, last_ref,
    out_ref, signals, responses, gathered,
):
    full = BLOCKS * SHARE
    turn_real, turn_imag = turn_ref[0], turn_ref[1]
    first = first_ref[0]
    signal = load_all(
        signals, jnp.concatenate([own_ref[:, : full // 2, :], other_ref[...]], axis=1)
    )
    response = load_all(responses, own_ref[:, full:, :])
    signal = turned_blocks(signal, first_ref[place_ref[2]], turn_real, turn_imag)
    signal = mm3_right(signal, second_ref)
    response = mm3_right(turned_blocks(response, first, turn_real, turn_imag), second_ref)
    sig_real, sig_imag = signal[:, :LANES], signal[:, LANES:]
    res_real, res_imag = response[:, :LANES], response[:, LANES:]
    product = jnp.concatenate(
        [sig_real * res_real - sig_imag * res_imag, sig_real * res_imag + sig_imag * res_real],
        axis=1,
    )
    back = mm3_right(product, back_ref)
    reals, imags = [], []
    for at in range(SHARE):
        real = back[at * LANES : (at + 1) * LANES, :LANES]
        imag = back[at * LANES : (at + 1) * LANES, LANES:]
        reals.append(real * turn_real + imag * turn_imag)
        imags.append(imag * turn_real - real * turn_imag)
    turned = jnp.concatenate(
        [jnp.concatenate(reals, axis=1), jnp.concatenate(imags, axis=1)], axis=0
    )
    result = mm3_left(last_ref, turned)
    for at in range(SHARE):
        gathered[pl.ds(at, LANES, stride=SHARE), :] = result[:, at * LANES : (at + 1) * LANES]
    result = gathered[: CTX * BLOCKS * SHARE, :]
    out_ref[...] = result.reshape(CTX, BLOCKS * SHARE, LANES).astype(BF16)


def add_products(d_high, place_ref, piece_refs, w_own_ref, w_other_ref, total, squares):
    high, along, core = place_ref[0], place_ref[1], place_ref[2]
    whole_refs, mid_refs = piece_refs[:3], piece_refs[3:]
    for d_along, ref in (*zip((0, YS - 1, 1), whole_refs), (2, None)):
        chip = lax.rem(high + d_high, HI) * YS + lax.rem(along + d_along, YS)
        scaled, weights = [], []
        for slot in range(CORES):
            block = mid_refs[slot][...] if ref is None else ref[slot]
            values = block[:HALF].astype(F32)
            squares = squares + values * values
            scaled.append((values * block[HALF:].astype(F32)[:1]).astype(BF16))
            owner = chip * CORES + (core if slot == 0 else 1 - core)
            start = pl.multiple_of(owner * LANES, LANES)
            weights.append(
                jnp.concatenate(
                    [w_own_ref[pl.ds(start, LANES), :], w_other_ref[pl.ds(start, LANES), :]],
                    axis=1,
                )
            )
        total = total + mm(jnp.concatenate(scaled, axis=1), jnp.concatenate(weights, axis=0))
    return total, squares


def near_kernel(place_ref, *refs):
    *piece_refs, w_own_ref, w_other_ref, total_ref, squares_ref = refs
    total_ref[...], squares_ref[...] = add_products(
        0,
        place_ref,
        piece_refs,
        w_own_ref,
        w_other_ref,
        jnp.zeros((HALF, 2 * LANES), F32),
        jnp.zeros((HALF, LANES), F32),
    )


def project_kernel(place_ref, *refs):
    *piece_refs, w_own_ref, w_other_ref, response_ref, total_ref, squares_ref, out_ref = refs
    count = HALF // LANES
    total, squares = add_products(
        1, place_ref, piece_refs, w_own_ref, w_other_ref, total_ref[...], squares_ref[...]
    )
    power = jnp.sum(squares, axis=1, keepdims=True) * (1.0 / FEATURES)
    total = total * lax.rsqrt(power + EPS)
    for slot in range(CORES):
        for pair in range(count // 2):
            parts = []
            for block in (2 * pair, 2 * pair + 1):
                part = total[
                    block * LANES : (block + 1) * LANES, slot * LANES : (slot + 1) * LANES
                ]
                parts.append(part.T.reshape(CTX, SHARE, LANES))
            start = (slot * count + 2 * pair) * SHARE
            out_ref[:, start : start + 2 * SHARE, :] = jnp.concatenate(parts, axis=1).astype(BF16)
    out_ref[:, BLOCKS * SHARE :, :] = response_ref[...]


def turn_kernel(blocks_ref, out_ref):
    for pair in range(BLOCKS // 2):
        values = blocks_ref[:, pair * 2 * SHARE : (pair + 1) * 2 * SHARE, :].astype(F32)
        for k in range(2):
            part = values[:, k * SHARE : (k + 1) * SHARE, :].reshape(LANES, LANES)
            start = (2 * pair + k) * LANES
            out_ref[start : start + LANES, :] = part.T.astype(BF16)


VMEM = pl.BlockSpec(memory_space=pltpu.VMEM)
SMEM = pl.BlockSpec(memory_space=pltpu.SMEM)
PARAMS = pltpu.CompilerParams(vmem_limit_bytes=48 * 1024 * 1024)


def call(kernel, outs, operands, scratch=(), first_spec=VMEM, flops=0):
    moved = sum(x.size * x.dtype.itemsize for x in operands)
    return pl.pallas_call(
        kernel,
        out_shape=outs,
        in_specs=[first_spec] + [VMEM] * (len(operands) - 1),
        out_specs=jax.tree.map(lambda _: VMEM, outs),
        scratch_shapes=list(scratch),
        compiler_params=PARAMS,
        cost_estimate=pl.CostEstimate(flops=flops, bytes_accessed=moved, transcendentals=0),
    )(*operands)


def bf16(*shape):
    return jax.ShapeDtypeStruct(shape, BF16)


def tp_shift(value, d_high, d_along, d_core):
    pairs = []
    for high in range(HI):
        for along in range(YS):
            for core in range(CORES):
                source = (high * YS + along) * CORES + core
                target = (
                    (high + d_high) % HI * YS + (along + d_along) % YS
                ) * CORES + (core + d_core) % CORES
                pairs.append((source, target))
    return lax.ppermute(value, "tp", pairs)


def gather(mine, theirs):
    def left(value):
        return tp_shift(value, 0, 1, 0)

    def right(value):
        return tp_shift(value, 0, YS - 1, 0)

    def ring(value):
        from_left, from_right = left(value), right(value)
        return [value, from_left, from_right, left(from_left[0]), right(from_right[1])]

    across = [tp_shift(mine, 1, 0, 0), tp_shift(theirs, 1, 0, 1)]
    own = jnp.stack([mine, tp_shift(theirs, 0, 0, 1)])
    return ring(own), ring(jnp.stack(across))


def on_device(tokens, gain, w_inputs, filters, w_plus, w_minus):
    table = tables()
    position = lax.axis_index("tp")
    core = lax.rem(position, CORES)
    place = jnp.stack(
        [position // (YS * CORES), lax.rem(position // CORES, YS), core, core]
    ).astype(jnp.int32)

    gain_rows = jnp.broadcast_to(gain[None, :], (PAD, LANES))
    mine, theirs = (
        jnp.concatenate(
            [lax.dynamic_slice_in_dim(tokens, half * HALF, HALF, axis=0), gain_rows], axis=0
        )
        for half in (core, 1 - core)
    )
    near, far = gather(mine, theirs)
    w_other = tp_shift(w_inputs, 0, 0, 1)

    lag_sign = 1.0 - 2.0 * (lax.iota(jnp.int32, ROWS) % 2).astype(F32)
    response = jnp.einsum("kt,kc->ct", filters, w_plus.astype(F32), precision=HIGHEST)
    response = response + lag_sign[None, :] * jnp.einsum(
        "kt,kc->ct", filters, w_minus.astype(F32), precision=HIGHEST
    )
    response = (
        response.reshape(CTX, SHARE, BLOCKS, LANES)
        .transpose(0, 2, 1, 3)
        .astype(BF16)
        .reshape(CTX, BLOCKS * SHARE, LANES)
    )

    flops = HALF * 2 * LANES * FEATURES
    total, squares = call(
        near_kernel,
        (
            jax.ShapeDtypeStruct((HALF, 2 * LANES), F32),
            jax.ShapeDtypeStruct((HALF, LANES), F32),
        ),
        [place, *near, w_inputs, w_other],
        first_spec=SMEM,
        flops=flops,
    )
    blocks = call(
        project_kernel,
        bf16(CTX, 2 * BLOCKS * SHARE, LANES),
        [place, *far, w_inputs, w_other, response, total, squares],
        first_spec=SMEM,
        flops=flops,
    )
    blocks = lax.all_to_all(blocks, "ctx", split_axis=0, concat_axis=0, tiled=True)
    other = tp_shift(blocks[:, BLOCKS * SHARE // 2 : BLOCKS * SHARE, :], 0, 0, 1)
    consts = [jnp.asarray(table[k]) for k in ("first", "turn", "second", "second_back", "last")]
    unpacked = pltpu.VMEM(((CTX * BLOCKS + 1) * SHARE, LANES), F32)
    mixed = call(
        mix_kernel,
        bf16(CTX, BLOCKS * SHARE, LANES),
        [place, blocks, other, *consts],
        [unpacked, unpacked, unpacked],
        first_spec=SMEM,
        flops=3 * 10**9,
    )
    mixed = lax.all_to_all(mixed, "ctx", split_axis=0, concat_axis=0, tiled=True)
    return call(turn_kernel, bf16(ROWS, LANES), [mixed])


def solution(mesh):
    in_specs = (
        P("ctx", "tp"),
        P("tp"),
        P(None, "tp"),
        P(None, "ctx"),
        P(None, "tp"),
        P(None, "tp"),
    )
    return jax.shard_map(
        on_device, mesh=mesh, in_specs=in_specs, out_specs=P("ctx", "tp"), check_vma=False
    )
```

```python
import math

import jax
import jax.numpy as jnp
import ml_dtypes
import numpy as np
from jax import lax
from jax.experimental import pallas as pl
from jax.experimental.pallas import tpu as pltpu
from jax.sharding import PartitionSpec as P

EPS = 1e-05
HIGHEST = lax.Precision.HIGHEST
CTX, HI, YS, CORES = 16, 2, 4, 2
LANES = 128
FEATURES = 2048
SHARE = 8
ROWS = 1024
HALF = ROWS // CORES
BLOCKS = ROWS // LANES
PAD = 16
BF16, F32 = jnp.bfloat16, jnp.float32


def split_high_low(table):
    high = table.astype(ml_dtypes.bfloat16)
    low = (table - high.astype(np.float64)).astype(ml_dtypes.bfloat16)
    return high, low


def tables():
    ids = np.arange(LANES)
    quarter = ids + 0.25
    outer = np.exp(-2j * np.pi * np.outer(quarter, ids) / LANES)
    first = np.concatenate([outer.real, outer.imag], axis=0)
    twiddle = np.exp(-2j * np.pi * np.outer(quarter, ids) / LANES**2)
    inner = np.exp(-2j * np.pi * np.outer(ids, ids) / LANES)
    second = np.block([[inner.real, inner.imag], [-inner.imag, inner.real]])
    other = (ids // BLOCKS) * BLOCKS + (ids % BLOCKS + BLOCKS // 2) % BLOCKS
    natural = np.concatenate(split_high_low(first), axis=1)
    swapped = np.concatenate(split_high_low(first[:, other]), axis=1)
    last = split_high_low(first.T / LANES**2)
    return dict(
        first=np.stack([natural, swapped]),
        turn=np.stack([twiddle.real, twiddle.imag]).astype(np.float32),
        second=np.stack(split_high_low(second)),
        second_back=np.stack(split_high_low(second.T)),
        last=np.stack(last),
    )


def mm(left, right):
    return jnp.dot(left, right, preferred_element_type=F32)


def high_low(value):
    high = value.astype(BF16)
    return high, (value - high.astype(F32)).astype(BF16)


def mm3_right(value, table):
    high, low = high_low(value)
    return mm(
        jnp.concatenate([high, low, high], axis=1),
        jnp.concatenate([table[0], table[0], table[1]], axis=0),
    )


def mm3_left(table, value):
    high, low = high_low(value)
    return mm(
        jnp.concatenate([table[0], table[0], table[1]], axis=1),
        jnp.concatenate([high, low, high], axis=0),
    )


def turned_blocks(values, first, turn_real, turn_imag):
    mixed = mm(first, jnp.concatenate([values, values], axis=0))
    rows = []
    for at in range(SHARE):
        real = mixed[:LANES, at * LANES : (at + 1) * LANES]
        imag = mixed[LANES:, at * LANES : (at + 1) * LANES]
        rows.append(
            jnp.concatenate(
                [real * turn_real - imag * turn_imag, real * turn_imag + imag * turn_real], axis=1
            )
        )
    return jnp.concatenate(rows, axis=0)


def load_all(unpacked, values):
    unpacked[: CTX * BLOCKS * SHARE, :] = values.astype(F32).reshape(CTX * BLOCKS * SHARE, LANES)
    return jnp.concatenate(
        [unpacked[pl.ds(at, LANES, stride=SHARE), :] for at in range(SHARE)], axis=1
    ).astype(BF16)


def mix_kernel(
    place_ref, own_ref, other_ref, first_ref, turn_ref, second_ref, back_ref, last_ref,
    out_ref, signals, responses, gathered,
):
    full = BLOCKS * SHARE
    turn_real, turn_imag = turn_ref[0], turn_ref[1]
    first = first_ref[0]
    signal = load_all(
        signals, jnp.concatenate([own_ref[:, : full // 2, :], other_ref[...]], axis=1)
    )
    response = load_all(responses, own_ref[:, full:, :])
    signal = turned_blocks(signal, first_ref[place_ref[2]], turn_real, turn_imag)
    signal = mm3_right(signal, second_ref)
    response = mm3_right(turned_blocks(response, first, turn_real, turn_imag), second_ref)
    sig_real, sig_imag = signal[:, :LANES], signal[:, LANES:]
    res_real, res_imag = response[:, :LANES], response[:, LANES:]
    product = jnp.concatenate(
        [sig_real * res_real - sig_imag * res_imag, sig_real * res_imag + sig_imag * res_real],
        axis=1,
    )
    back = mm3_right(product, back_ref)
    reals, imags = [], []
    for at in range(SHARE):
        real = back[at * LANES : (at + 1) * LANES, :LANES]
        imag = back[at * LANES : (at + 1) * LANES, LANES:]
        reals.append(real * turn_real + imag * turn_imag)
        imags.append(imag * turn_real - real * turn_imag)
    turned = jnp.concatenate(
        [jnp.concatenate(reals, axis=1), jnp.concatenate(imags, axis=1)], axis=0
    )
    result = mm3_left(last_ref, turned)
    for at in range(SHARE):
        gathered[pl.ds(at, LANES, stride=SHARE), :] = result[:, at * LANES : (at + 1) * LANES]
    result = gathered[: CTX * BLOCKS * SHARE, :]
    out_ref[...] = result.reshape(CTX, BLOCKS * SHARE, LANES).astype(BF16)


def add_products(d_high, place_ref, piece_refs, w_own_ref, w_other_ref, total, squares):
    high, along, core = place_ref[0], place_ref[1], place_ref[2]
    whole_refs, mid_refs = piece_refs[:3], piece_refs[3:]
    for d_along, ref in (*zip((0, YS - 1, 1), whole_refs), (2, None)):
        chip = lax.rem(high + d_high, HI) * YS + lax.rem(along + d_along, YS)
        scaled, weights = [], []
        for slot in range(CORES):
            block = mid_refs[slot][...] if ref is None else ref[slot]
            values = block[:HALF].astype(F32)
            squares = squares + values * values
            scaled.append((values * block[HALF:].astype(F32)[:1]).astype(BF16))
            owner = chip * CORES + (core if slot == 0 else 1 - core)
            start = pl.multiple_of(owner * LANES, LANES)
            weights.append(
                jnp.concatenate(
                    [w_own_ref[pl.ds(start, LANES), :], w_other_ref[pl.ds(start, LANES), :]],
                    axis=1,
                )
            )
        total = total + mm(jnp.concatenate(scaled, axis=1), jnp.concatenate(weights, axis=0))
    return total, squares


def near_kernel(place_ref, *refs):
    *piece_refs, w_own_ref, w_other_ref, total_ref, squares_ref = refs
    total_ref[...], squares_ref[...] = add_products(
        0,
        place_ref,
        piece_refs,
        w_own_ref,
        w_other_ref,
        jnp.zeros((HALF, 2 * LANES), F32),
        jnp.zeros((HALF, LANES), F32),
    )


def project_kernel(place_ref, *refs):
    *piece_refs, w_own_ref, w_other_ref, response_ref, total_ref, squares_ref, out_ref = refs
    count = HALF // LANES
    total, squares = add_products(
        1, place_ref, piece_refs, w_own_ref, w_other_ref, total_ref[...], squares_ref[...]
    )
    power = jnp.sum(squares, axis=1, keepdims=True) * (1.0 / FEATURES)
    total = total * lax.rsqrt(power + EPS)
    for slot in range(CORES):
        for pair in range(count // 2):
            parts = []
            for block in (2 * pair, 2 * pair + 1):
                part = total[
                    block * LANES : (block + 1) * LANES, slot * LANES : (slot + 1) * LANES
                ]
                parts.append(part.T.reshape(CTX, SHARE, LANES))
            start = (slot * count + 2 * pair) * SHARE
            out_ref[:, start : start + 2 * SHARE, :] = jnp.concatenate(parts, axis=1).astype(BF16)
    out_ref[:, BLOCKS * SHARE :, :] = response_ref[...]


def turn_kernel(blocks_ref, out_ref):
    for pair in range(BLOCKS // 2):
        values = blocks_ref[:, pair * 2 * SHARE : (pair + 1) * 2 * SHARE, :].astype(F32)
        for k in range(2):
            part = values[:, k * SHARE : (k + 1) * SHARE, :].reshape(LANES, LANES)
            start = (2 * pair + k) * LANES
            out_ref[start : start + LANES, :] = part.T.astype(BF16)


VMEM = pl.BlockSpec(memory_space=pltpu.VMEM)
SMEM = pl.BlockSpec(memory_space=pltpu.SMEM)
PARAMS = pltpu.CompilerParams(vmem_limit_bytes=48 * 1024 * 1024)


def call(kernel, outs, operands, scratch=(), first_spec=VMEM, flops=0):
    moved = sum(x.size * x.dtype.itemsize for x in operands)
    return pl.pallas_call(
        kernel,
        out_shape=outs,
        in_specs=[first_spec] + [VMEM] * (len(operands) - 1),
        out_specs=jax.tree.map(lambda _: VMEM, outs),
        scratch_shapes=list(scratch),
        compiler_params=PARAMS,
        cost_estimate=pl.CostEstimate(flops=flops, bytes_accessed=moved, transcendentals=0),
    )(*operands)


def half_kernel(value_ref, out_ref):
    rows = BLOCKS * SHARE // 2
    out_ref[...] = value_ref[:, rows : 2 * rows, :]


def bf16(*shape):
    return jax.ShapeDtypeStruct(shape, BF16)


def tp_shift(value, d_high, d_along, d_core):
    pairs = []
    for high in range(HI):
        for along in range(YS):
            for core in range(CORES):
                source = (high * YS + along) * CORES + core
                target = (
                    (high + d_high) % HI * YS + (along + d_along) % YS
                ) * CORES + (core + d_core) % CORES
                pairs.append((source, target))
    return lax.ppermute(value, "tp", pairs)


def gather(mine, theirs):
    def left(value):
        return tp_shift(value, 0, 1, 0)

    def right(value):
        return tp_shift(value, 0, YS - 1, 0)

    def ring(value):
        from_left, from_right = left(value), right(value)
        return [value, from_left, from_right, left(from_left[0]), right(from_right[1])]

    across = [tp_shift(mine, 1, 0, 0), tp_shift(theirs, 1, 0, 1)]
    own = jnp.stack([mine, tp_shift(theirs, 0, 0, 1)])
    return ring(own), ring(jnp.stack(across))


def on_device(tokens, gain, w_inputs, filters, w_plus, w_minus):
    table = tables()
    position = lax.axis_index("tp")
    core = lax.rem(position, CORES)
    place = jnp.stack(
        [position // (YS * CORES), lax.rem(position // CORES, YS), core, core]
    ).astype(jnp.int32)

    gain_rows = jnp.broadcast_to(gain[None, :], (PAD, LANES))
    mine, theirs = (
        jnp.concatenate(
            [lax.dynamic_slice_in_dim(tokens, half * HALF, HALF, axis=0), gain_rows], axis=0
        )
        for half in (core, 1 - core)
    )
    near, far = gather(mine, theirs)
    w_other = tp_shift(w_inputs, 0, 0, 1)

    lag_sign = 1.0 - 2.0 * (lax.iota(jnp.int32, ROWS) % 2).astype(F32)
    response = jnp.einsum("kt,kc->ct", filters, w_plus.astype(F32), precision=HIGHEST)
    response = response + lag_sign[None, :] * jnp.einsum(
        "kt,kc->ct", filters, w_minus.astype(F32), precision=HIGHEST
    )
    response = (
        response.reshape(CTX, SHARE, BLOCKS, LANES)
        .transpose(0, 2, 1, 3)
        .astype(BF16)
        .reshape(CTX, BLOCKS * SHARE, LANES)
    )

    flops = HALF * 2 * LANES * FEATURES
    total, squares = call(
        near_kernel,
        (
            jax.ShapeDtypeStruct((HALF, 2 * LANES), F32),
            jax.ShapeDtypeStruct((HALF, LANES), F32),
        ),
        [place, *near, w_inputs, w_other],
        first_spec=SMEM,
        flops=flops,
    )
    blocks = call(
        project_kernel,
        bf16(CTX, 2 * BLOCKS * SHARE, LANES),
        [place, *far, w_inputs, w_other, response, total, squares],
        first_spec=SMEM,
        flops=flops,
    )
    blocks = lax.all_to_all(blocks, "ctx", split_axis=0, concat_axis=0, tiled=True)
    other = tp_shift(call(half_kernel, bf16(CTX, BLOCKS * SHARE // 2, LANES), [blocks]), 0, 0, 1)
    consts = [jnp.asarray(table[k]) for k in ("first", "turn", "second", "second_back", "last")]
    unpacked = pltpu.VMEM(((CTX * BLOCKS + 1) * SHARE, LANES), F32)
    mixed = call(
        mix_kernel,
        bf16(CTX, BLOCKS * SHARE, LANES),
        [place, blocks, other, *consts],
        [unpacked, unpacked, unpacked],
        first_spec=SMEM,
        flops=3 * 10**9,
    )
    mixed = lax.all_to_all(mixed, "ctx", split_axis=0, concat_axis=0, tiled=True)
    return call(turn_kernel, bf16(ROWS, LANES), [mixed])


def solution(mesh):
    in_specs = (
        P("ctx", "tp"),
        P("tp"),
        P(None, "tp"),
        P(None, "ctx"),
        P(None, "tp"),
        P(None, "tp"),
    )
    return jax.shard_map(
        on_device, mesh=mesh, in_specs=in_specs, out_specs=P("ctx", "tp"), check_vma=False
    )
```

```python
import math

import jax
import jax.numpy as jnp
import ml_dtypes
import numpy as np
from jax import lax
from jax.experimental import pallas as pl
from jax.experimental.pallas import tpu as pltpu
from jax.sharding import PartitionSpec as P

EPS = 1e-05
HIGHEST = lax.Precision.HIGHEST
CTX, HI, YS, CORES = 16, 2, 4, 2
LANES = 128
FEATURES = 2048
SHARE = 8
ROWS = 1024
HALF = ROWS // CORES
BLOCKS = ROWS // LANES
PAD = 16
BF16, F32 = jnp.bfloat16, jnp.float32


def split_high_low(table):
    high = table.astype(ml_dtypes.bfloat16)
    low = (table - high.astype(np.float64)).astype(ml_dtypes.bfloat16)
    return high, low


def tables():
    ids = np.arange(LANES)
    quarter = ids + 0.25
    outer = np.exp(-2j * np.pi * np.outer(quarter, ids) / LANES)
    first = np.concatenate([outer.real, outer.imag], axis=0)
    twiddle = np.exp(-2j * np.pi * np.outer(quarter, ids) / LANES**2)
    inner = np.exp(-2j * np.pi * np.outer(ids, ids) / LANES)
    second = np.block([[inner.real, inner.imag], [-inner.imag, inner.real]])
    other = (ids // BLOCKS) * BLOCKS + (ids % BLOCKS + BLOCKS // 2) % BLOCKS
    natural = np.concatenate(split_high_low(first), axis=1)
    swapped = np.concatenate(split_high_low(first[:, other]), axis=1)
    last = split_high_low(first.T / LANES**2)
    return dict(
        first=np.stack([natural, swapped]),
        turn=np.stack([twiddle.real, twiddle.imag]).astype(np.float32),
        second=np.stack(split_high_low(second)),
        second_back=np.stack(split_high_low(second.T)),
        last=np.stack(last),
    )


def mm(left, right):
    return jnp.dot(left, right, preferred_element_type=F32)


def high_low(value):
    high = value.astype(BF16)
    return high, (value - high.astype(F32)).astype(BF16)


def mm3_right(value, table):
    high, low = high_low(value)
    return mm(
        jnp.concatenate([high, low, high], axis=1),
        jnp.concatenate([table[0], table[0], table[1]], axis=0),
    )


def mm3_left(table, value):
    high, low = high_low(value)
    return mm(
        jnp.concatenate([table[0], table[0], table[1]], axis=1),
        jnp.concatenate([high, low, high], axis=0),
    )


def turned_blocks(values, first, turn_real, turn_imag):
    mixed = mm(first, jnp.concatenate([values, values], axis=0))
    rows = []
    for at in range(SHARE):
        real = mixed[:LANES, at * LANES : (at + 1) * LANES]
        imag = mixed[LANES:, at * LANES : (at + 1) * LANES]
        rows.append(
            jnp.concatenate(
                [real * turn_real - imag * turn_imag, real * turn_imag + imag * turn_real], axis=1
            )
        )
    return jnp.concatenate(rows, axis=0)


def load_all(unpacked, values):
    unpacked[: CTX * BLOCKS * SHARE, :] = values.astype(F32).reshape(CTX * BLOCKS * SHARE, LANES)
    return jnp.concatenate(
        [unpacked[pl.ds(at, LANES, stride=SHARE), :] for at in range(SHARE)], axis=1
    ).astype(BF16)


def mix_kernel(
    place_ref, own_ref, other_ref, first_ref, turn_ref, second_ref, back_ref, last_ref,
    out_ref, signals, responses, gathered,
):
    full = BLOCKS * SHARE
    turn_real, turn_imag = turn_ref[0], turn_ref[1]
    first = first_ref[0]
    signal = load_all(
        signals, jnp.concatenate([own_ref[:, : full // 2, :], other_ref[...]], axis=1)
    )
    response = load_all(responses, own_ref[:, full:, :])
    signal = turned_blocks(signal, first_ref[place_ref[2]], turn_real, turn_imag)
    signal = mm3_right(signal, second_ref)
    response = mm3_right(turned_blocks(response, first, turn_real, turn_imag), second_ref)
    sig_real, sig_imag = signal[:, :LANES], signal[:, LANES:]
    res_real, res_imag = response[:, :LANES], response[:, LANES:]
    product = jnp.concatenate(
        [sig_real * res_real - sig_imag * res_imag, sig_real * res_imag + sig_imag * res_real],
        axis=1,
    )
    back = mm3_right(product, back_ref)
    reals, imags = [], []
    for at in range(SHARE):
        real = back[at * LANES : (at + 1) * LANES, :LANES]
        imag = back[at * LANES : (at + 1) * LANES, LANES:]
        reals.append(real * turn_real + imag * turn_imag)
        imags.append(imag * turn_real - real * turn_imag)
    turned = jnp.concatenate(
        [jnp.concatenate(reals, axis=1), jnp.concatenate(imags, axis=1)], axis=0
    )
    result = mm3_left(last_ref, turned)
    for at in range(SHARE):
        gathered[pl.ds(at, LANES, stride=SHARE), :] = result[:, at * LANES : (at + 1) * LANES]
    result = gathered[: CTX * BLOCKS * SHARE, :]
    out_ref[...] = result.reshape(CTX, BLOCKS * SHARE, LANES).astype(BF16)


def add_products(d_high, place_ref, piece_refs, w_own_ref, w_other_ref, total, squares):
    high, along, core = place_ref[0], place_ref[1], place_ref[2]
    whole_refs, mid_refs = piece_refs[:3], piece_refs[3:]
    for d_along, ref in (*zip((0, YS - 1, 1), whole_refs), (2, None)):
        chip = lax.rem(high + d_high, HI) * YS + lax.rem(along + d_along, YS)
        scaled, weights = [], []
        for slot in range(CORES):
            block = mid_refs[slot][...] if ref is None else ref[slot]
            values = block[:HALF].astype(F32)
            squares = squares + values * values
            scaled.append((values * block[HALF:].astype(F32)[:1]).astype(BF16))
            owner = chip * CORES + (core if slot == 0 else 1 - core)
            start = pl.multiple_of(owner * LANES, LANES)
            weights.append(
                jnp.concatenate(
                    [w_own_ref[pl.ds(start, LANES), :], w_other_ref[pl.ds(start, LANES), :]],
                    axis=1,
                )
            )
        total = total + mm(jnp.concatenate(scaled, axis=1), jnp.concatenate(weights, axis=0))
    return total, squares


def near_kernel(place_ref, *refs):
    *piece_refs, w_own_ref, w_other_ref, total_ref, squares_ref = refs
    total_ref[...], squares_ref[...] = add_products(
        0,
        place_ref,
        piece_refs,
        w_own_ref,
        w_other_ref,
        jnp.zeros((HALF, 2 * LANES), F32),
        jnp.zeros((HALF, LANES), F32),
    )


def project_kernel(place_ref, *refs):
    *piece_refs, w_own_ref, w_other_ref, response_ref, total_ref, squares_ref, out_ref = refs
    count = HALF // LANES
    total, squares = add_products(
        1, place_ref, piece_refs, w_own_ref, w_other_ref, total_ref[...], squares_ref[...]
    )
    power = jnp.sum(squares, axis=1, keepdims=True) * (1.0 / FEATURES)
    total = total * lax.rsqrt(power + EPS)
    for slot in range(CORES):
        for pair in range(count // 2):
            parts = []
            for block in (2 * pair, 2 * pair + 1):
                part = total[
                    block * LANES : (block + 1) * LANES, slot * LANES : (slot + 1) * LANES
                ]
                parts.append(part.T.reshape(CTX, SHARE, LANES))
            start = (slot * count + 2 * pair) * SHARE
            out_ref[:, start : start + 2 * SHARE, :] = jnp.concatenate(parts, axis=1).astype(BF16)
    out_ref[:, BLOCKS * SHARE :, :] = response_ref[...]


def turn_kernel(blocks_ref, out_ref):
    for pair in range(BLOCKS // 2):
        values = blocks_ref[:, pair * 2 * SHARE : (pair + 1) * 2 * SHARE, :].astype(F32)
        for k in range(2):
            part = values[:, k * SHARE : (k + 1) * SHARE, :].reshape(LANES, LANES)
            start = (2 * pair + k) * LANES
            out_ref[start : start + LANES, :] = part.T.astype(BF16)


VMEM = pl.BlockSpec(memory_space=pltpu.VMEM)
SMEM = pl.BlockSpec(memory_space=pltpu.SMEM)
PARAMS = pltpu.CompilerParams(vmem_limit_bytes=48 * 1024 * 1024)


def call(kernel, outs, operands, scratch=(), first_spec=VMEM, flops=0):
    moved = sum(x.size * x.dtype.itemsize for x in operands)
    return pl.pallas_call(
        kernel,
        out_shape=outs,
        in_specs=[first_spec] + [VMEM] * (len(operands) - 1),
        out_specs=jax.tree.map(lambda _: VMEM, outs),
        scratch_shapes=list(scratch),
        compiler_params=PARAMS,
        cost_estimate=pl.CostEstimate(flops=flops, bytes_accessed=moved, transcendentals=0),
    )(*operands)


def half_kernel(value_ref, out_ref):
    rows = BLOCKS * SHARE // 2
    out_ref[...] = value_ref[:, rows : 2 * rows, :]


def bf16(*shape):
    return jax.ShapeDtypeStruct(shape, BF16)


def tp_shift(value, d_high, d_along, d_core):
    pairs = []
    for high in range(HI):
        for along in range(YS):
            for core in range(CORES):
                source = (high * YS + along) * CORES + core
                target = (
                    (high + d_high) % HI * YS + (along + d_along) % YS
                ) * CORES + (core + d_core) % CORES
                pairs.append((source, target))
    return lax.ppermute(value, "tp", pairs)


def gather(mine, theirs):
    def left(value):
        return tp_shift(value, 0, 1, 0)

    def right(value):
        return tp_shift(value, 0, YS - 1, 0)

    def ring(value):
        from_right = right(value)
        second = right(from_right[1])
        from_left = left(value)
        return [value, from_left, from_right, left(from_left[0]), second]

    across = [tp_shift(mine, 1, 0, 0), tp_shift(theirs, 1, 0, 1)]
    own = jnp.stack([mine, tp_shift(theirs, 0, 0, 1)])
    return ring(own), ring(jnp.stack(across))


def on_device(tokens, gain, w_inputs, filters, w_plus, w_minus):
    table = tables()
    position = lax.axis_index("tp")
    core = lax.rem(position, CORES)
    place = jnp.stack(
        [position // (YS * CORES), lax.rem(position // CORES, YS), core, core]
    ).astype(jnp.int32)

    gain_rows = jnp.broadcast_to(gain[None, :], (PAD, LANES))
    mine, theirs = (
        jnp.concatenate(
            [lax.dynamic_slice_in_dim(tokens, half * HALF, HALF, axis=0), gain_rows], axis=0
        )
        for half in (core, 1 - core)
    )
    near, far = gather(mine, theirs)
    w_other = tp_shift(w_inputs, 0, 0, 1)

    lag_sign = 1.0 - 2.0 * (lax.iota(jnp.int32, ROWS) % 2).astype(F32)
    response = jnp.einsum("kt,kc->ct", filters, w_plus.astype(F32), precision=HIGHEST)
    response = response + lag_sign[None, :] * jnp.einsum(
        "kt,kc->ct", filters, w_minus.astype(F32), precision=HIGHEST
    )
    response = (
        response.reshape(CTX, SHARE, BLOCKS, LANES)
        .transpose(0, 2, 1, 3)
        .astype(BF16)
        .reshape(CTX, BLOCKS * SHARE, LANES)
    )

    flops = HALF * 2 * LANES * FEATURES
    total, squares = call(
        near_kernel,
        (
            jax.ShapeDtypeStruct((HALF, 2 * LANES), F32),
            jax.ShapeDtypeStruct((HALF, LANES), F32),
        ),
        [place, *near, w_inputs, w_other],
        first_spec=SMEM,
        flops=flops,
    )
    blocks = call(
        project_kernel,
        bf16(CTX, 2 * BLOCKS * SHARE, LANES),
        [place, *far, w_inputs, w_other, response, total, squares],
        first_spec=SMEM,
        flops=flops,
    )
    blocks = lax.all_to_all(blocks, "ctx", split_axis=0, concat_axis=0, tiled=True)
    other = tp_shift(call(half_kernel, bf16(CTX, BLOCKS * SHARE // 2, LANES), [blocks]), 0, 0, 1)
    consts = [jnp.asarray(table[k]) for k in ("first", "turn", "second", "second_back", "last")]
    unpacked = pltpu.VMEM(((CTX * BLOCKS + 1) * SHARE, LANES), F32)
    mixed = call(
        mix_kernel,
        bf16(CTX, BLOCKS * SHARE, LANES),
        [place, blocks, other, *consts],
        [unpacked, unpacked, unpacked],
        first_spec=SMEM,
        flops=3 * 10**9,
    )
    mixed = lax.all_to_all(mixed, "ctx", split_axis=0, concat_axis=0, tiled=True)
    return call(turn_kernel, bf16(ROWS, LANES), [mixed])


def solution(mesh):
    in_specs = (
        P("ctx", "tp"),
        P("tp"),
        P(None, "tp"),
        P(None, "ctx"),
        P(None, "tp"),
        P(None, "tp"),
    )
    return jax.shard_map(
        on_device, mesh=mesh, in_specs=in_specs, out_specs=P("ctx", "tp"), check_vma=False
    )
```
